32 devices in a mesh: parts: 2 (over y), seq: 8 (over z, x), head: 2 (over core).
Axes of the slice: x: 2, y: 2, z: 4, core: 2. Of those that a mesh axis runs over, the one named last changes fastest.
Arguments:
- queries: bfloat16 [2048, 4096], P(('parts', 'seq', 'head')), parts along dimension 0, may hold values from -0.59765625 to 0.59765625
- keys: bfloat16 [2048, 4096], P(('parts', 'seq', 'head')), parts along dimension 0, may hold values from -0.59765625 to 0.59765625
- values: bfloat16 [2048, 4096], P(('parts', 'seq', 'head')), parts along dimension 0, may hold values from -0.59765625 to 0.59765625
- out_grad: bfloat16 [2048, 4096], P(('parts', 'seq', 'head')), parts along dimension 0, may hold values from -0.59765625 to 0.59765625
- decay_log: bfloat16 [2048, 32], P(('parts', 'seq', 'head')), parts along dimension 0, may hold values from -1 to 0, as said below
Outputs:
- grad_q: bfloat16 [2048, 4096], P(('parts', 'seq', 'head')), parts along dimension 0
- grad_k: bfloat16 [2048, 4096], P(('parts', 'seq', 'head')), parts along dimension 0
- grad_v: bfloat16 [2048, 4096], P(('parts', 'seq', 'head')), parts along dimension 0
The draws below stay inside these ranges and needn't reach their ends.
There are 2 independent parts, one for each index of `parts`. The reference program is written for one: setup_inputs(seed, part) draws one part's arguments, and reference() takes and returns one part's arrays. A program takes and returns all parts, laid end to end along the dimension named above; each array names one. Nothing has to cross between parts.
Inputs may be any that keep to these rules, and one draw needn't show every extreme that they name: `decay_log`: negative everywhere.
All inputs are finite; a program needn't handle non-finite values.
Results may differ from the reference program's by a relative error of at most 0.0058.
Values may be sent and summed in bfloat16 or wider, within the bound.
A program may use at most 64 MiB of HBM per device.

```python
import jax
import jax.numpy as jnp
from jax import lax

HEAD_COUNT = 32
DH = 128
BLK = 64
SEQUENCE_LENGTH = 1024


def draw_decay_log(key, part):
    rapid_key, gradual_key, speedy_key, token_key, block_key, location_key, spike_key = jax.random.split(key, 7)
    share = 0.5
    fast = jax.random.uniform(rapid_key, (HEAD_COUNT,)) < share
    slow_rate = jnp.exp(jax.random.uniform(gradual_key, (HEAD_COUNT,), jnp.float32, jnp.log(0.05), jnp.log(0.5))) / SEQUENCE_LENGTH
    fast_rate = jnp.exp(jax.random.uniform(speedy_key, (HEAD_COUNT,), jnp.float32, jnp.log(1.0 / 50), jnp.log(1.0 / 20)))
    decay_rate = jnp.where(fast, fast_rate, slow_rate)
    token_jitter = jnp.exp(jax.random.uniform(token_key, (SEQUENCE_LENGTH, HEAD_COUNT), jnp.float32, -0.7, 0.7))
    block_jitter = jnp.exp(jax.random.uniform(block_key, (SEQUENCE_LENGTH // BLK, HEAD_COUNT), jnp.float32, -0.7, 0.7))
    block_jitter = jnp.repeat(block_jitter, BLK, axis=0)
    spots = jax.random.randint(location_key, (2, HEAD_COUNT), 0, SEQUENCE_LENGTH)
    places = jnp.arange(SEQUENCE_LENGTH)[:, None, None]
    struck_positions = jnp.any(places == spots[None], axis=1)
    sudden_spike = jnp.log(jax.random.uniform(spike_key, (SEQUENCE_LENGTH, HEAD_COUNT), jnp.float32, 0.5, 0.8))
    decay_factor = -decay_rate[None, :] * token_jitter * block_jitter + jnp.where(struck_positions, sudden_spike, 0.0)
    return decay_factor.astype(jnp.bfloat16)


def shard_levels(own_key, shape, cuts, low, largest):
    gain, own = 1.0, jax.random.fold_in(own_key, 6)
    for dim, blocks in cuts:
        steps = jnp.exp(jax.random.uniform(jax.random.fold_in(own, dim), (blocks,), jnp.float32, low / len(cuts), largest / len(cuts)))
        gain = gain * jnp.repeat(steps, shape[dim] // blocks).reshape([-1 if axis == dim else 1 for axis in range(len(shape))])
    return gain


def scatter_about(rng, extent, spread, most, cuts=(), kind=jnp.bfloat16):
    result = spread * jax.random.normal(rng, extent, jnp.float32)
    if cuts:
        result = result * shard_levels(rng, extent, cuts, -0.22, 0.18)
    return jnp.clip(result, -most, most).astype(kind)


def setup_inputs(seed: int = 0, part: int = 0) -> dict:
    streams_of = jax.random.split(jax.random.key(seed), 6)
    part_splits = jax.random.split(jax.random.fold_in(streams_of[5], part), 6)
    return {
        "queries": scatter_about(part_splits[0], (SEQUENCE_LENGTH, HEAD_COUNT * DH), 0.09, 0.59765625, ((0, 16),)),
        "keys": scatter_about(part_splits[1], (SEQUENCE_LENGTH, HEAD_COUNT * DH), 0.09, 0.59765625, ((0, 16),)),
        "values": scatter_about(part_splits[2], (SEQUENCE_LENGTH, HEAD_COUNT * DH), 0.09, 0.59765625, ((0, 16),)),
        "out_grad": scatter_about(part_splits[3], (SEQUENCE_LENGTH, HEAD_COUNT * DH), 0.09, 0.59765625, ((0, 16),)),
        "decay_log": draw_decay_log(jax.random.fold_in(jax.random.fold_in(streams_of[5], part), 71), part),
    }


def rounded(array):
    return lax.optimization_barrier(array.astype(jnp.bfloat16)).astype(jnp.float32)


def block_parts(queries, keys, values, out_grad, decay_factor):
    cumul = jnp.cumsum(decay_factor, axis=0)
    ending = cumul[-1]
    keep = jnp.exp(ending[None, :] - cumul)
    rising = jnp.exp(cumul)
    q_full = queries.astype(jnp.float32)
    k_full = keys.astype(jnp.float32)
    v_full = values.astype(jnp.float32)
    o_full = out_grad.astype(jnp.float32)
    weighted_v = rounded(v_full * keep[..., None])
    kv_block = jnp.einsum('thi,thj->hij', k_full, weighted_v)
    weighted_q = rounded(q_full * rising[..., None])
    qo_block = jnp.einsum('thi,thj->hij', weighted_q, o_full)
    trans = cumul.T
    diff = trans[:, :, None] - trans[:, None, :]
    lower = jnp.arange(BLK)[:, None] >= jnp.arange(BLK)[None, :]
    mask = jnp.where(lower[None], jnp.exp(jnp.minimum(diff, 0.0)), 0.0)
    vscore = rounded(jnp.einsum('thd,shd->hts', o_full, v_full) * mask)
    qscore = rounded(jnp.einsum('thd,shd->hts', q_full, k_full) * mask)
    local_q = jnp.einsum('hts,shd->thd', vscore, k_full)
    local_k = jnp.einsum('hts,thd->shd', vscore, q_full)
    local_v = jnp.einsum('hts,thd->shd', qscore, o_full)
    return jnp.exp(ending), kv_block, qo_block, rising, keep, local_q, local_k, local_v


def reference(queries, keys, values, out_grad, decay_log):
    blocks = SEQUENCE_LENGTH // BLK

    def split_point(array):
        return array.reshape(blocks, BLK, HEAD_COUNT, DH)

    inputs = (split_point(queries), split_point(keys), split_point(values), split_point(out_grad),
              decay_log.astype(jnp.float32).reshape(blocks, BLK, HEAD_COUNT))

    def forward(state, pieces):
        factor, kv_block, qo_block, rising, keep, local_q, local_k, local_v = block_parts(*pieces)
        grad = local_q + rising[..., None] * jnp.einsum('thj,hij->thi', pieces[3].astype(jnp.float32), rounded(state))
        return factor[:, None, None] * state + kv_block, grad.astype(jnp.bfloat16)

    def backward(suffix, pieces):
        factor, kv_block, qo_block, rising, keep, local_q, local_k, local_v = block_parts(*pieces)
        carried = rounded(suffix)
        grad_k = local_k + keep[..., None] * jnp.einsum('shj,hij->shi', pieces[2].astype(jnp.float32), carried)
        grad_v = local_v + keep[..., None] * jnp.einsum('shi,hij->shj', pieces[1].astype(jnp.float32), carried)
        return qo_block + factor[:, None, None] * suffix, (grad_k.astype(jnp.bfloat16), grad_v.astype(jnp.bfloat16))

    start = jnp.zeros((HEAD_COUNT, DH, DH), jnp.float32)
    unused, grad_q = lax.scan(forward, start, inputs)
    unused_back, grads = lax.scan(backward, start, inputs, reverse=True)
    shape = (SEQUENCE_LENGTH, HEAD_COUNT * DH)
    return grad_q.reshape(shape), grads[0].reshape(shape), grads[1].reshape(shape)
```

```python
import functools

import jax
import jax.numpy as jnp
from jax import lax
from jax.experimental import pallas as pl
from jax.experimental.pallas import tpu as pltpu
from jax.sharding import PartitionSpec as P

MESH = pl.DeviceIdType.MESH
F32 = jnp.float32
BF16 = jnp.bfloat16
NT = (((1,), (1,)), ((), ()))
NN = (((1,), (0,)), ((), ()))
TN = (((0,), (0,)), ((), ()))


def mm(a, b, dims):
    return lax.dot_general(a, b, dims, preferred_element_type=F32)


def kernel(
    sizes, q_ref, k_ref, v_ref, o_ref, dec_ref, gq_ref, gk_ref, gv_ref,
    x, dec, cum_b, cum_t, coef, kvqo, a_in, a_out, l_in, l_out, h_in, h_out, local, grads,
    in_own, in_send, in_recv, dec_own, dec_send, dec_recv,
    a_send, a_recv, l_send, l_recv, h_send, h_recv, out_own, out_send, out_recv,
):
    rows_n, cols_n, cores, heads, dh, per, pieces, lag = sizes
    chunks = heads // per
    blk = q_ref.shape[0]
    span = cores * blk
    half = heads * dh
    width = per * dh
    piece = half // pieces
    wire = a_in.dtype
    seq = lax.axis_index("seq")
    core = lax.axis_index("head")
    row, col = seq // cols_n, seq % cols_n
    group = cols_n * cores
    slot = col * cores + core
    sources = (k_ref, v_ref, q_ref, o_ref)

    def sides(d):
        rr = jnp.where(d == 0, row, rows_n - 1 - row)
        cc = jnp.where(d == 0, col, cols_n - 1 - col)
        return rr, cc, 1 - 2 * d

    def place(target):
        return {"seq": row * cols_n + target // cores, "head": target % cores}

    def columns(owner, start, size):
        return pl.ds(pl.multiple_of(owner * half + start, dh), size)

    def own_copy(a, p):
        return pltpu.make_async_copy(
            sources[a].at[:, columns(core, p * piece, piece)],
            x.at[a, core, :, columns(0, p * piece, piece)],
            in_own.at[a, p],
        )

    def in_copy(a, p, j):
        other = (core + j) % cores
        return pltpu.make_async_remote_copy(
            sources[a].at[:, columns(other, p * piece, piece)],
            x.at[a, core, :, columns(0, p * piece, piece)],
            in_send.at[j - 1, a, p], in_recv.at[j - 1, a, p],
            device_id={"head": other}, device_id_type=MESH,
        )

    def dec_copy(j):
        return pltpu.make_async_remote_copy(
            dec_ref, dec.at[slot], dec_send.at[j - 1], dec_recv.at[j - 1],
            device_id=place((slot + j) % group), device_id_type=MESH,
        )

    def hop(src, dst, send, recv, d, g, target):
        return pltpu.make_async_remote_copy(
            src.at[d, g], dst.at[d, g], send.at[d, g], recv.at[d, g],
            device_id={"seq": target}, device_id_type=MESH,
        )

    def a_copy(d, g):
        return hop(a_out, a_in, a_send, a_recv, d, g, seq + (1 - 2 * d) * cols_n)

    def l_copy(d, g):
        return hop(l_out, l_in, l_send, l_recv, d, g, seq + (1 - 2 * d))

    def h_copy(d, g, src):
        return hop(src, h_in, h_send, h_recv, d, g, seq - (1 - 2 * d))

    outs = (gq_ref, gk_ref, gv_ref)

    def out_copy(n, g):
        return pltpu.make_async_copy(
            grads.at[n, core, :, columns(0, g * width, width)],
            outs[n].at[:, columns(core, g * width, width)],
            out_own.at[n, g],
        )

    def back_copy(n, g, j):
        other = (core + j) % cores
        return pltpu.make_async_remote_copy(
            grads.at[n, other, :, columns(0, g * width, width)],
            outs[n].at[:, columns(core, g * width, width)],
            out_send.at[j - 1, n, g], out_recv.at[j - 1, n, g],
            device_id={"head": other}, device_id_type=MESH,
        )

    def head_rows(a, index):
        cut = x[a, :, :, pl.ds(pl.multiple_of(index * dh, dh), dh)]
        return cut.reshape(span, dh)

    own_dec = pltpu.make_async_copy(dec_ref, dec.at[slot], dec_own)
    own_dec.start()
    barrier = pltpu.get_barrier_semaphore()
    for j in range(1, group):
        pl.semaphore_signal(barrier, inc=1, device_id=place((slot + j) % group), device_id_type=MESH)

    @pl.when(row > 0)
    def _():
        pl.semaphore_signal(barrier, inc=1, device_id={"seq": seq - cols_n}, device_id_type=MESH)

    @pl.when(row < rows_n - 1)
    def _():
        pl.semaphore_signal(barrier, inc=1, device_id={"seq": seq + cols_n}, device_id_type=MESH)

    for p in range(pieces):
        for a in range(4):
            own_copy(a, p).start()

    for d in range(2):
        rr, cc, _ = sides(d)

        @pl.when(rr == 0)
        def _():
            a_in[d] = jnp.zeros_like(a_in[d])

        @pl.when(cc == 0)
        def _():
            l_in[d] = jnp.zeros_like(l_in[d])

        @pl.when(jnp.logical_or(cc == cols_n - 1, rr == 0))
        def _():
            h_in[d] = jnp.zeros_like(h_in[d])

    peers = group - 1 + jnp.where(row > 0, 1, 0) + jnp.where(row < rows_n - 1, 1, 0)
    pl.semaphore_wait(barrier, peers)

    for j in range(1, group):
        dec_copy(j).start()
    for p in range(pieces):
        for a in range(4):
            for j in range(1, cores):
                in_copy(a, p, j).start()
    own_dec.wait()
    for j in range(1, group):
        dec_copy(j).wait_recv()

    def mine(array, axis):
        result = lax.slice_in_dim(array, 0, heads, axis=axis)
        for j in range(1, cores):
            part = lax.slice_in_dim(array, j * heads, (j + 1) * heads, axis=axis)
            result = jnp.where(core == j, part, result)
        return result

    t_index = lax.broadcasted_iota(jnp.int32, (span, span), 0)
    s_index = lax.broadcasted_iota(jnp.int32, (span, span), 1)
    tri = jnp.where(t_index >= s_index, 1.0, 0.0).astype(BF16)
    logs = dec[pl.ds(col * cores, cores)].reshape(span, dec.shape[2])
    cum = mine(mm(tri, logs, NN), 1)
    cum_row = mine(mm(logs, tri, (((0,), (1,)), ((), ()))), 0)
    zero = jnp.zeros((1, dec.shape[2]), F32)
    before, own, after = zero, zero, zero
    for other in range(cols_n):
        total = zero
        for j in range(cores):
            total += jnp.sum(dec[other * cores + j].astype(F32), axis=0, keepdims=True)
        before += jnp.where(other < col, total, 0.0)
        own += jnp.where(other == col, total, 0.0)
        after += jnp.where(other > col, total, 0.0)
    kinds = [mine(k, 1) for k in (own, before + own + after, before, after)]
    for i in range(heads):
        cum_b[i] = jnp.broadcast_to(cum[:, i : i + 1], (span, dh))
        cum_t[i] = cum_row[i : i + 1, :]
        for n, kind in enumerate(kinds):
            coef[n, i] = jnp.exp(jnp.broadcast_to(kind[:, i : i + 1], (8, dh)))

    def rate(n, index):
        return coef[n, index, 0:1, :]

    def row_step(d, g):
        rr, cc, _ = sides(d)

        @pl.when(rr > 0)
        def _():
            a_copy(d, g).wait_recv()

        @pl.when(rr < rows_n - 1)
        def _():
            for j in range(per):
                index = g * per + j
                a = a_in[d, g, j].astype(F32)
                a_out[d, g, j] = (rate(1, index) * a + rate(3 - d, index) * kvqo[d, index]).astype(wire)
            a_copy(d, g).start()

        if cols_n > 1:

            @pl.when(cc == 0)
            def _():
                for j in range(per):
                    index = g * per + j
                    a = a_in[d, g, j].astype(F32)
                    l_out[d, g, j] = (rate(0, index) * a + kvqo[d, index]).astype(wire)
                l_copy(d, g).start()

            @pl.when(jnp.logical_and(cc == cols_n - 1, rr > 0))
            def _():
                h_copy(d, g, a_in).start()

    def col_step(d, g):
        rr, cc, _ = sides(d)
        if cols_n > 1:

            @pl.when(cc > 0)
            def _():
                l_copy(d, g).wait_recv()

        if cols_n > 2:

            @pl.when(jnp.logical_and(cc > 0, cc < cols_n - 1))
            def _():
                for j in range(per):
                    index = g * per + j
                    a = l_in[d, g, j].astype(F32) + rate(2 + d, index) * a_in[d, g, j].astype(F32)
                    l_out[d, g, j] = (rate(0, index) * a + kvqo[d, index]).astype(wire)
                l_copy(d, g).start()

        if cols_n > 1:

            @pl.when(jnp.logical_and(cc < cols_n - 1, rr > 0))
            def _():
                h_copy(d, g, h_out).wait_recv()

        if cols_n > 2:

            @pl.when(jnp.logical_and(jnp.logical_and(cc > 0, cc < cols_n - 1), rr > 0))
            def _():
                for j in range(per):
                    h_out[d, g, j] = (h_in[d, g, j].astype(F32) + a_in[d, g, j].astype(F32)).astype(wire)
                h_copy(d, g, h_out).start()

    def carried(d, g, j):
        index = g * per + j
        both = a_in[d, g, j].astype(F32) + h_in[d, g, j].astype(F32)
        return (l_in[d, g, j].astype(F32) + rate(2 + d, index) * both).astype(BF16)

    def first(g, _):
        @pl.when(g % (chunks // pieces) == 0)
        def _():
            p = g // (chunks // pieces)
            for a in range(4):
                own_copy(a, p).wait()
                for j in range(1, cores):
                    in_copy(a, p, j).wait_recv()

        for j in range(per):
            index = g * per + j
            cum_h = cum_b[index]
            keep = jnp.exp(cum_h[span - 1 : span, :] - cum_h)
            rising = jnp.exp(cum_h)
            weighted_v = (head_rows(1, index).astype(F32) * keep).astype(BF16)
            weighted_q = (head_rows(2, index).astype(F32) * rising).astype(BF16)
            kvqo[0, index] = mm(head_rows(0, index), weighted_v, TN)
            kvqo[1, index] = mm(weighted_q, head_rows(3, index), TN)
        for d in range(2):

            @pl.when(sides(d)[0] == 0)
            def _():
                row_step(d, g)

        return 0

    lax.fori_loop(0, chunks, first, 0)

    def within(g):
        lower = lax.broadcasted_iota(jnp.int32, (span, span), 0) >= lax.broadcasted_iota(
            jnp.int32, (span, span), 1
        )
        for j in range(per):
            index = g * per + j
            k, v, q, o = (head_rows(a, index) for a in range(4))
            mask = jnp.where(lower, jnp.exp(jnp.minimum(cum_b[index] - cum_t[index], 0.0)), 0.0)
            vscore = (mm(o, v, NT) * mask).astype(BF16)
            qscore = (mm(q, k, NT) * mask).astype(BF16)
            local[0, index] = mm(vscore, k, NN)
            local[1, index] = mm(vscore, q, TN)
            local[2, index] = mm(qscore, o, TN)

    def last(g):
        for d in range(2):
            col_step(d, g)
        for j in range(per):
            index = g * per + j
            state = carried(0, g, j)
            suffix = carried(1, g, j)
            cum_h = cum_b[index]
            keep = jnp.exp(cum_h[span - 1 : span, :] - cum_h)
            rising = jnp.exp(cum_h)
            found = (
                local[0, index] + rising * mm(head_rows(3, index), state, NT),
                local[1, index] + keep * mm(head_rows(1, index), suffix, NT),
                local[2, index] + keep * mm(head_rows(0, index), suffix, NN),
            )
            for n in range(3):
                place_at = pl.ds(pl.multiple_of(index * dh, dh), dh)
                grads[n, :, :, place_at] = found[n].astype(BF16).reshape(cores, blk, dh)
        for n in range(3):
            for j in range(1, cores):
                back_copy(n, g, j).start()
            out_copy(n, g).start()

    upper = jnp.where(2 * row >= rows_n, 1, 0)

    def second(g, _):
        @pl.when(g < chunks)
        def _():
            for i in range(2):
                d = (upper + i) % 2

                @pl.when(sides(d)[0] > 0)
                def _():
                    row_step(d, g)

            within(g)

        @pl.when(g >= lag)
        def _():
            last(g - lag)

        return 0

    lax.fori_loop(0, chunks + lag, second, 0)

    for j in range(1, group):
        dec_copy(j).wait_send()
    for p in range(pieces):
        for a in range(4):
            for j in range(1, cores):
                in_copy(a, p, j).wait_send()

    def close(g, _):
        for d in range(2):
            rr, cc, _ = sides(d)

            @pl.when(rr < rows_n - 1)
            def _():
                a_copy(d, g).wait_send()

            if cols_n > 1:

                @pl.when(cc < cols_n - 1)
                def _():
                    l_copy(d, g).wait_send()

                @pl.when(jnp.logical_and(cc > 0, rr > 0))
                def _():
                    h_copy(d, g, h_out).wait_send()

        for n in range(3):
            out_copy(n, g).wait()
            for j in range(1, cores):
                back_copy(n, g, j).wait_send()
                back_copy(n, g, j).wait_recv()
        return 0

    lax.fori_loop(0, chunks, close, 0)


def solution(mesh):
    count, cores = mesh.shape["seq"], mesh.shape["head"]
    cols_n = max(c for c in range(1, count + 1) if count % c == 0 and c * c <= count)
    rows_n = count // cols_n
    wire = BF16 if rows_n + cols_n <= 8 else F32

    def per_device(queries, keys, values, out_grad, decay_log):
        blk, model = queries.shape
        all_heads = decay_log.shape[1]
        heads, dh = all_heads // cores, model // all_heads
        per, pieces, lag = 2, 4, 2
        chunks = heads // per
        span, group = cores * blk, cols_n * cores
        sizes = (rows_n, cols_n, cores, heads, dh, per, pieces, lag)
        states = pltpu.VMEM((2, chunks, per, dh, dh), wire)
        pair = pltpu.SemaphoreType.DMA((2, chunks))
        return pl.pallas_call(
            functools.partial(kernel, sizes),
            out_shape=[jax.ShapeDtypeStruct((blk, model), BF16)] * 3,
            in_specs=[pl.BlockSpec(memory_space=pl.ANY)] * 5,
            out_specs=[pl.BlockSpec(memory_space=pl.ANY)] * 3,
            scratch_shapes=[
                pltpu.VMEM((4, cores, blk, heads * dh), BF16),
                pltpu.VMEM((group, blk, all_heads), BF16),
                pltpu.VMEM((heads, span, dh), F32),
                pltpu.VMEM((heads, 1, span), F32),
                pltpu.VMEM((4, heads, 8, dh), F32),
                pltpu.VMEM((2, heads, dh, dh), F32),
                states, states, states, states, states, states,
                pltpu.VMEM((3, heads, span, dh), F32),
                pltpu.VMEM((3, cores, blk, heads * dh), BF16),
                pltpu.SemaphoreType.DMA((4, pieces)),
                pltpu.SemaphoreType.DMA((cores - 1, 4, pieces)),
                pltpu.SemaphoreType.DMA((cores - 1, 4, pieces)),
                pltpu.SemaphoreType.DMA,
                pltpu.SemaphoreType.DMA((group - 1,)),
                pltpu.SemaphoreType.DMA((group - 1,)),
                pair, pair, pair, pair, pair, pair,
                pltpu.SemaphoreType.DMA((3, chunks)),
                pltpu.SemaphoreType.DMA((cores - 1, 3, chunks)),
                pltpu.SemaphoreType.DMA((cores - 1, 3, chunks)),
            ],
            compiler_params=pltpu.CompilerParams(
                collective_id=0, has_side_effects=True, vmem_limit_bytes=48 * 1024 * 1024
            ),
            cost_estimate=pl.CostEstimate(
                flops=20 * heads * span * dh * dh, bytes_accessed=14 * blk * model, transcendentals=0
            ),
        )(queries, keys, values, out_grad, decay_log)

    rows = P(("parts", "seq", "head"), None)
    return jax.shard_map(
        per_device, mesh=mesh, in_specs=(rows,) * 5, out_specs=(rows,) * 3, check_vma=False
    )
```

```python
import functools

import jax
import jax.numpy as jnp
from jax import lax
from jax.experimental import pallas as pl
from jax.experimental.pallas import tpu as pltpu
from jax.sharding import PartitionSpec as P

MESH = pl.DeviceIdType.MESH
F32 = jnp.float32
BF16 = jnp.bfloat16
NT = (((1,), (1,)), ((), ()))
NN = (((1,), (0,)), ((), ()))
TN = (((0,), (0,)), ((), ()))


def mm(a, b, dims):
    return lax.dot_general(a, b, dims, preferred_element_type=F32)


def kernel(
    sizes, q_ref, k_ref, v_ref, o_ref, dec_ref, gq_ref, gk_ref, gv_ref,
    x, dec, cum_b, cum_t, coef, kvqo, a_in, a_out, l_in, l_out, h_in, h_out, local, grads,
    in_own, in_send, in_recv, dec_own, dec_send, dec_recv,
    a_send, a_recv, l_send, l_recv, h_send, h_recv, out_own, out_send, out_recv,
):
    rows_n, cols_n, cores, heads, dh, per, pieces, behind, lag, paired = sizes
    chunks = heads // per
    late = chunks - paired
    blk = q_ref.shape[0]
    span = cores * blk
    half = heads * dh
    width = per * dh
    piece = half // pieces
    wire = a_in.dtype
    seq = lax.axis_index("seq")
    core = lax.axis_index("head")
    row, col = seq // cols_n, seq % cols_n
    group = cols_n * cores
    slot = col * cores + core
    sources = (k_ref, v_ref, q_ref, o_ref)

    def sides(d):
        rr = jnp.where(d == 0, row, rows_n - 1 - row)
        cc = jnp.where(d == 0, col, cols_n - 1 - col)
        return rr, cc, 1 - 2 * d

    def place(target):
        return {"seq": row * cols_n + target // cores, "head": target % cores}

    def columns(owner, start, size):
        return pl.ds(pl.multiple_of(owner * half + start, dh), size)

    def own_copy(a, p):
        return pltpu.make_async_copy(
            sources[a].at[:, columns(core, p * piece, piece)],
            x.at[a, core, :, columns(0, p * piece, piece)],
            in_own.at[a, p],
        )

    def in_copy(a, p, j):
        other = (core + j) % cores
        return pltpu.make_async_remote_copy(
            sources[a].at[:, columns(other, p * piece, piece)],
            x.at[a, core, :, columns(0, p * piece, piece)],
            in_send.at[j - 1, a, p], in_recv.at[j - 1, a, p],
            device_id={"head": other}, device_id_type=MESH,
        )

    def dec_copy(j):
        return pltpu.make_async_remote_copy(
            dec_ref, dec.at[slot], dec_send.at[j - 1], dec_recv.at[j - 1],
            device_id=place((slot + j) % group), device_id_type=MESH,
        )

    def hop(src, dst, send, recv, d, g, target):
        return pltpu.make_async_remote_copy(
            src.at[d, g], dst.at[d, g], send.at[d, g], recv.at[d, g],
            device_id={"seq": target}, device_id_type=MESH,
        )

    def a_copy(d, g):
        return hop(a_out, a_in, a_send, a_recv, d, g, seq + (1 - 2 * d) * cols_n)

    def l_copy(d, g):
        return hop(l_out, l_in, l_send, l_recv, d, g, seq + (1 - 2 * d))

    def h_copy(d, g, src):
        return hop(src, h_in, h_send, h_recv, d, g, seq - (1 - 2 * d))

    outs = (gq_ref, gk_ref, gv_ref)

    def out_copy(n, g):
        return pltpu.make_async_copy(
            grads.at[n, core, :, columns(0, g * width, width)],
            outs[n].at[:, columns(core, g * width, width)],
            out_own.at[n, g],
        )

    def back_copy(n, g, j):
        other = (core + j) % cores
        return pltpu.make_async_remote_copy(
            grads.at[n, other, :, columns(0, g * width, width)],
            outs[n].at[:, columns(core, g * width, width)],
            out_send.at[j - 1, n, g], out_recv.at[j - 1, n, g],
            device_id={"head": other}, device_id_type=MESH,
        )

    def head_rows(a, index):
        cut = x[a, :, :, pl.ds(pl.multiple_of(index * dh, dh), dh)]
        return cut.reshape(span, dh)

    own_dec = pltpu.make_async_copy(dec_ref, dec.at[slot], dec_own)
    own_dec.start()
    barrier = pltpu.get_barrier_semaphore()
    for j in range(1, group):
        pl.semaphore_signal(barrier, inc=1, device_id=place((slot + j) % group), device_id_type=MESH)

    @pl.when(row > 0)
    def _():
        pl.semaphore_signal(barrier, inc=1, device_id={"seq": seq - cols_n}, device_id_type=MESH)

    @pl.when(row < rows_n - 1)
    def _():
        pl.semaphore_signal(barrier, inc=1, device_id={"seq": seq + cols_n}, device_id_type=MESH)

    order = [(p + late * pieces // chunks) % pieces for p in range(pieces)]
    for p in order:
        for a in range(4):
            own_copy(a, p).start()

    for d in range(2):
        rr, cc, _ = sides(d)

        @pl.when(rr == 0)
        def _():
            a_in[d] = jnp.zeros_like(a_in[d])

        @pl.when(cc == 0)
        def _():
            l_in[d] = jnp.zeros_like(l_in[d])

        @pl.when(jnp.logical_or(cc == cols_n - 1, rr == 0))
        def _():
            h_in[d, :late] = jnp.zeros_like(h_in[d, :late])

    peers = group - 1 + jnp.where(row > 0, 1, 0) + jnp.where(row < rows_n - 1, 1, 0)
    pl.semaphore_wait(barrier, peers)

    for j in range(1, group):
        dec_copy(j).start()
    for p in order:
        for a in range(4):
            for j in range(1, cores):
                in_copy(a, p, j).start()
    own_dec.wait()
    for j in range(1, group):
        dec_copy(j).wait_recv()

    def mine(array, axis):
        result = lax.slice_in_dim(array, 0, heads, axis=axis)
        for j in range(1, cores):
            part = lax.slice_in_dim(array, j * heads, (j + 1) * heads, axis=axis)
            result = jnp.where(core == j, part, result)
        return result

    cum = cum_row = 0.0
    for j in range(cores):
        t_index = lax.broadcasted_iota(jnp.int32, (span, blk), 0)
        s_index = lax.broadcasted_iota(jnp.int32, (span, blk), 1) + j * blk
        tri = jnp.where(t_index >= s_index, 1.0, 0.0).astype(BF16)
        logs = dec[col * cores + j]
        cum += mm(tri, logs, NT)
        cum_row += mm(logs, tri, NT)
    cum, cum_row = mine(cum, 1), mine(cum_row, 0)
    ones = jnp.ones((span, blk), BF16)
    zero = jnp.zeros((dec.shape[1], span), F32)
    before, own, after = zero, zero, zero
    for other in range(cols_n):
        total = zero
        for j in range(cores):
            total += mm(dec[other * cores + j], ones, NT)
        before += jnp.where(other < col, total, 0.0)
        own += jnp.where(other == col, total, 0.0)
        after += jnp.where(other > col, total, 0.0)
    kinds = [jnp.exp(mine(k, 0)) for k in (own, before + own + after, before, after)]
    for i in range(heads):
        cum_b[i] = jnp.broadcast_to(cum[:, i : i + 1], (span, dh))
        cum_t[i] = cum_row[i : i + 1, :]
        for n, kind in enumerate(kinds):
            coef[n, i] = kind[i : i + 1, :]

    def rate(n, index):
        return coef[n, index]

    def row_step(d, g):
        rr, cc, _ = sides(d)

        @pl.when(rr > 0)
        def _():
            a_copy(d, g).wait_recv()

        @pl.when(g < late)
        def _():
            @pl.when(rr < rows_n - 1)
            def _():
                for j in range(per):
                    index = g * per + j
                    a = a_in[d, g, j].astype(F32)
                    a_out[d, g, j] = (rate(1, index) * a + rate(3 - d, index) * kvqo[d, index]).astype(wire)
                a_copy(d, g).start()

            if cols_n > 1:

                @pl.when(cc == 0)
                def _():
                    for j in range(per):
                        index = g * per + j
                        a = a_in[d, g, j].astype(F32)
                        l_out[d, g, j] = (rate(0, index) * a + kvqo[d, index]).astype(wire)
                    l_copy(d, g).start()

                @pl.when(jnp.logical_and(cc == cols_n - 1, rr > 0))
                def _():
                    h_copy(d, g, a_in).start()

        if paired:
            @pl.when(g >= late)
            def _():
                @pl.when(cc > 0)
                def _():
                    l_copy(d, g).wait_recv()

                @pl.when(jnp.logical_and(cc == 0, rr < rows_n - 1))
                def _():
                    h_copy(d, g, h_out).wait_recv()

                @pl.when(rr < rows_n - 1)
                def _():
                    for j in range(per):
                        index = g * per + j
                        met = jnp.where(
                            cc == 0, h_in[d, g, j].astype(F32), rate(0, index) * l_in[d, g, j].astype(F32)
                        )
                        grown = rate(1, index) * a_in[d, g, j].astype(F32) + rate(3 - d, index) * kvqo[d, index]
                        a_out[d, g, j] = (grown + met).astype(wire)
                    a_copy(d, g).start()

    def meet(d, g):
        rr, cc, _ = sides(d)

        @pl.when(cc == 0)
        def _():
            for j in range(per):
                l_out[d, g, j] = kvqo[d, g * per + j].astype(wire)
            l_copy(d, g).start()

        @pl.when(jnp.logical_and(cc > 0, rr < rows_n - 1))
        def _():
            for j in range(per):
                h_out[d, g, j] = kvqo[d, g * per + j].astype(wire)
            h_copy(d, g, h_out).start()

    def col_step(d, g):
        rr, cc, _ = sides(d)
        if cols_n > 1:

            @pl.when(cc > 0)
            def _():
                l_copy(d, g).wait_recv()

        if cols_n > 2:

            @pl.when(jnp.logical_and(cc > 0, cc < cols_n - 1))
            def _():
                for j in range(per):
                    index = g * per + j
                    a = l_in[d, g, j].astype(F32) + rate(2 + d, index) * a_in[d, g, j].astype(F32)
                    l_out[d, g, j] = (rate(0, index) * a + kvqo[d, index]).astype(wire)
                l_copy(d, g).start()

        if cols_n > 1:

            @pl.when(jnp.logical_and(cc < cols_n - 1, rr > 0))
            def _():
                h_copy(d, g, h_out).wait_recv()

        if cols_n > 2:

            @pl.when(jnp.logical_and(jnp.logical_and(cc > 0, cc < cols_n - 1), rr > 0))
            def _():
                for j in range(per):
                    h_out[d, g, j] = (h_in[d, g, j].astype(F32) + a_in[d, g, j].astype(F32)).astype(wire)
                h_copy(d, g, h_out).start()

    def carried(d, g, j):
        index = g * per + j
        both = a_in[d, g, j].astype(F32) + jnp.where(g < late, h_in[d, g, j].astype(F32), 0.0)
        return (l_in[d, g, j].astype(F32) + rate(2 + d, index) * both).astype(BF16)

    def first(i, _):
        g = (i + late) % chunks

        @pl.when(g % (chunks // pieces) == 0)
        def _():
            p = g // (chunks // pieces)
            for a in range(4):
                own_copy(a, p).wait()
                for j in range(1, cores):
                    in_copy(a, p, j).wait_recv()

        for j in range(per):
            index = g * per + j
            cum_h = cum_b[index]
            keep = jnp.exp(cum_h[span - 1 : span, :] - cum_h)
            rising = jnp.exp(cum_h)
            weighted_v = (head_rows(1, index).astype(F32) * keep).astype(BF16)
            weighted_q = (head_rows(2, index).astype(F32) * rising).astype(BF16)
            kvqo[0, index] = mm(head_rows(0, index), weighted_v, TN)
            kvqo[1, index] = mm(weighted_q, head_rows(3, index), TN)
        for d in range(2):

            @pl.when(jnp.logical_and(sides(d)[0] == 0, g < late))
            def _():
                row_step(d, g)

            if paired:

                @pl.when(g >= late)
                def _():
                    meet(d, g)

        return 0

    lax.fori_loop(0, chunks, first, 0)

    def within(g):
        lower = lax.broadcasted_iota(jnp.int32, (span, span), 0) >= lax.broadcasted_iota(
            jnp.int32, (span, span), 1
        )
        for j in range(per):
            index = g * per + j
            k, v, q, o = (head_rows(a, index) for a in range(4))
            mask = jnp.where(lower, jnp.exp(jnp.minimum(cum_b[index] - cum_t[index], 0.0)), 0.0)
            vscore = (mm(o, v, NT) * mask).astype(BF16)
            qscore = (mm(q, k, NT) * mask).astype(BF16)
            local[0, index] = mm(vscore, k, NN)
            local[1, index] = mm(vscore, q, TN)
            local[2, index] = mm(qscore, o, TN)

    def sent(g):
        for d in range(2):
            rr, cc, _ = sides(d)

            @pl.when(rr < rows_n - 1)
            def _():
                a_copy(d, g).wait_send()

            if cols_n > 1:

                @pl.when(cc < cols_n - 1)
                def _():
                    l_copy(d, g).wait_send()

                @pl.when(jnp.logical_and(cc > 0, jnp.where(g < late, rr > 0, rr < rows_n - 1)))
                def _():
                    h_copy(d, g, h_out).wait_send()

    def close(g, _):
        for n in range(3):
            out_copy(n, g).wait()
            for j in range(1, cores):
                back_copy(n, g, j).wait_send()
                back_copy(n, g, j).wait_recv()
        return 0

    def last(g):
        @pl.when(g < late)
        def _():
            for d in range(2):
                col_step(d, g)

        sent(g)
        for j in range(per):
            index = g * per + j
            state = carried(0, g, j)
            suffix = carried(1, g, j)
            cum_h = cum_b[index]
            keep = jnp.exp(cum_h[span - 1 : span, :] - cum_h)
            rising = jnp.exp(cum_h)
            found = (
                local[0, index] + rising * mm(head_rows(3, index), state, NT),
                local[1, index] + keep * mm(head_rows(1, index), suffix, NT),
                local[2, index] + keep * mm(head_rows(0, index), suffix, NN),
            )
            for n in range(3):
                place_at = pl.ds(pl.multiple_of(index * dh, dh), dh)
                grads[n, :, :, place_at] = found[n].astype(BF16).reshape(cores, blk, dh)
        for n in range(3):
            for j in range(1, cores):
                back_copy(n, g, j).start()
            out_copy(n, g).start()

        @pl.when(g >= 2)
        def _():
            close(g - 2, 0)

    def open_chain(g, _):
        for d in range(2):

            @pl.when(sides(d)[0] == 0)
            def _():
                row_step(d, g)

        return 0

    if paired:
        lax.fori_loop(late, chunks, open_chain, 0)
    upper = jnp.where(2 * row >= rows_n, 1, 0)

    def second(g, _):
        for i in range(2):
            d = (upper + i) % 2
            at = g - i * behind

            @pl.when(jnp.logical_and(sides(d)[0] > 0, jnp.logical_and(at >= 0, at < chunks)))
            def _():
                row_step(d, at)

        @pl.when(g < chunks)
        def _():
            within(g)

        @pl.when(g >= lag)
        def _():
            last(g - lag)

        return 0

    for j in range(1, group):
        dec_copy(j).wait_send()
    for p in range(pieces):
        for a in range(4):
            for j in range(1, cores):
                in_copy(a, p, j).wait_send()
    lax.fori_loop(0, chunks + lag, second, 0)

    lax.fori_loop(jnp.maximum(chunks - 2, 0), chunks, close, 0)


def solution(mesh):
    count, cores = mesh.shape["seq"], mesh.shape["head"]
    cols_n = max(c for c in range(1, count + 1) if count % c == 0 and c * c <= count)
    rows_n = count // cols_n
    wire = BF16 if rows_n + cols_n <= 8 else F32

    def per_device(queries, keys, values, out_grad, decay_log):
        blk, model = queries.shape
        all_heads = decay_log.shape[1]
        heads, dh = all_heads // cores, model // all_heads
        per, pieces, behind, lag = 2, 4, 2, 8
        paired = 2 if cols_n == 2 else 0
        chunks = heads // per
        span, group = cores * blk, cols_n * cores
        sizes = (rows_n, cols_n, cores, heads, dh, per, pieces, behind, lag, paired)
        states = pltpu.VMEM((2, chunks, per, dh, dh), wire)
        pair = pltpu.SemaphoreType.DMA((2, chunks))
        return pl.pallas_call(
            functools.partial(kernel, sizes),
            out_shape=[jax.ShapeDtypeStruct((blk, model), BF16)] * 3,
            in_specs=[pl.BlockSpec(memory_space=pl.ANY)] * 5,
            out_specs=[pl.BlockSpec(memory_space=pl.ANY)] * 3,
            scratch_shapes=[
                pltpu.VMEM((4, cores, blk, heads * dh), BF16),
                pltpu.VMEM((group, all_heads, blk), BF16),
                pltpu.VMEM((heads, span, dh), F32),
                pltpu.VMEM((heads, 1, span), F32),
                pltpu.VMEM((4, heads, 1, span), F32),
                pltpu.VMEM((2, heads, dh, dh), F32),
                states, states, states, states, states, states,
                pltpu.VMEM((3, heads, span, dh), F32),
                pltpu.VMEM((3, cores, blk, heads * dh), BF16),
                pltpu.SemaphoreType.DMA((4, pieces)),
                pltpu.SemaphoreType.DMA((cores - 1, 4, pieces)),
                pltpu.SemaphoreType.DMA((cores - 1, 4, pieces)),
                pltpu.SemaphoreType.DMA,
                pltpu.SemaphoreType.DMA((group - 1,)),
                pltpu.SemaphoreType.DMA((group - 1,)),
                pair, pair, pair, pair, pair, pair,
                pltpu.SemaphoreType.DMA((3, chunks)),
                pltpu.SemaphoreType.DMA((cores - 1, 3, chunks)),
                pltpu.SemaphoreType.DMA((cores - 1, 3, chunks)),
            ],
            compiler_params=pltpu.CompilerParams(
                collective_id=0, has_side_effects=True, vmem_limit_bytes=63 * 1024 * 1024
            ),
            cost_estimate=pl.CostEstimate(
                flops=20 * heads * span * dh * dh, bytes_accessed=14 * blk * model, transcendentals=0
            ),
        )(queries, keys, values, out_grad, decay_log.T)

    rows = P(("parts", "seq", "head"), None)
    return jax.shard_map(
        per_device, mesh=mesh, in_specs=(rows,) * 5, out_specs=(rows,) * 3, check_vma=False
    )
```

```python
import functools

import jax
import jax.numpy as jnp
from jax import lax
from jax.experimental import pallas as pl
from jax.experimental.pallas import tpu as pltpu
from jax.sharding import PartitionSpec as P

MESH = pl.DeviceIdType.MESH
F32 = jnp.float32
BF16 = jnp.bfloat16
NT = (((1,), (1,)), ((), ()))
NN = (((1,), (0,)), ((), ()))
TN = (((0,), (0,)), ((), ()))


def mm(a, b, dims):
    return lax.dot_general(a, b, dims, preferred_element_type=F32)


def kernel(
    sizes, q_ref, k_ref, v_ref, o_ref, dec_ref, gq_ref, gk_ref, gv_ref,
    x, dec, cum_b, cum_t, rise, kept, coef, kvqo, a_in, a_out, l_in, l_out, h_in, h_out, local, grads,
    in_own, in_send, in_recv, dec_own, dec_send, dec_recv,
    a_send, a_recv, l_send, l_recv, h_send, h_recv, out_own, out_send, out_recv,
):
    rows_n, cols_n, cores, heads, dh, per, pieces, behind, lag, paired = sizes
    chunks = heads // per
    late = chunks - paired
    joint = 2 if chunks % 2 == 0 else 1
    blk = q_ref.shape[0]
    span = cores * blk
    half = heads * dh
    width = per * dh
    piece = half // pieces
    wire = a_in.dtype
    seq = lax.axis_index("seq")
    core = lax.axis_index("head")
    row, col = seq // cols_n, seq % cols_n
    group = cols_n * cores
    slot = col * cores + core
    sources = (k_ref, v_ref, q_ref, o_ref)

    def sides(d):
        rr = jnp.where(d == 0, row, rows_n - 1 - row)
        cc = jnp.where(d == 0, col, cols_n - 1 - col)
        return rr, cc, 1 - 2 * d

    def place(target):
        return {"seq": row * cols_n + target // cores, "head": target % cores}

    def columns(owner, start, size):
        return pl.ds(pl.multiple_of(owner * half + start, dh), size)

    def own_copy(a, p):
        return pltpu.make_async_copy(
            sources[a].at[:, columns(core, p * piece, piece)],
            x.at[a, core, :, columns(0, p * piece, piece)],
            in_own.at[a, p],
        )

    def in_copy(a, p, j):
        other = (core + j) % cores
        return pltpu.make_async_remote_copy(
            sources[a].at[:, columns(other, p * piece, piece)],
            x.at[a, core, :, columns(0, p * piece, piece)],
            in_send.at[j - 1, a, p], in_recv.at[j - 1, a, p],
            device_id={"head": other}, device_id_type=MESH,
        )

    def dec_copy(j):
        return pltpu.make_async_remote_copy(
            dec_ref, dec.at[slot], dec_send.at[j - 1], dec_recv.at[j - 1],
            device_id=place((slot + j) % group), device_id_type=MESH,
        )

    def hop(src, dst, send, recv, d, g, target):
        return pltpu.make_async_remote_copy(
            src.at[d, g], dst.at[d, g], send.at[d, g], recv.at[d, g],
            device_id={"seq": target}, device_id_type=MESH,
        )

    def a_copy(d, g):
        return hop(a_out, a_in, a_send, a_recv, d, g, seq + (1 - 2 * d) * cols_n)

    def l_copy(d, g):
        return hop(l_out, l_in, l_send, l_recv, d, g, seq + (1 - 2 * d))

    def h_copy(d, g, src):
        return hop(src, h_in, h_send, h_recv, d, g, seq - (1 - 2 * d))

    outs = (gq_ref, gk_ref, gv_ref)

    def out_copy(n, g):
        return pltpu.make_async_copy(
            grads.at[n, core, :, columns(0, g * joint * width, joint * width)],
            outs[n].at[:, columns(core, g * joint * width, joint * width)],
            out_own.at[n, g],
        )

    def back_copy(n, g, j):
        other = (core + j) % cores
        return pltpu.make_async_remote_copy(
            grads.at[n, other, :, columns(0, g * joint * width, joint * width)],
            outs[n].at[:, columns(core, g * joint * width, joint * width)],
            out_send.at[j - 1, n, g], out_recv.at[j - 1, n, g],
            device_id={"head": other}, device_id_type=MESH,
        )

    def head_rows(a, index):
        cut = x[a, :, :, pl.ds(pl.multiple_of(index * dh, dh), dh)]
        return cut.reshape(span, dh)

    own_dec = pltpu.make_async_copy(dec_ref, dec.at[slot], dec_own)
    own_dec.start()
    barrier = pltpu.get_barrier_semaphore()
    for j in range(1, group):
        pl.semaphore_signal(barrier, inc=1, device_id=place((slot + j) % group), device_id_type=MESH)

    @pl.when(row > 0)
    def _():
        pl.semaphore_signal(barrier, inc=1, device_id={"seq": seq - cols_n}, device_id_type=MESH)

    @pl.when(row < rows_n - 1)
    def _():
        pl.semaphore_signal(barrier, inc=1, device_id={"seq": seq + cols_n}, device_id_type=MESH)

    order = [(p + late * pieces // chunks) % pieces for p in range(pieces)]
    for p in order:
        for a in range(4):
            own_copy(a, p).start()

    for d in range(2):
        rr, cc, _ = sides(d)

        @pl.when(rr == 0)
        def _():
            a_in[d] = jnp.zeros_like(a_in[d])

        @pl.when(cc == 0)
        def _():
            l_in[d] = jnp.zeros_like(l_in[d])

        @pl.when(jnp.logical_or(cc == cols_n - 1, rr == 0))
        def _():
            h_in[d, :late] = jnp.zeros_like(h_in[d, :late])

    peers = group - 1 + jnp.where(row > 0, 1, 0) + jnp.where(row < rows_n - 1, 1, 0)
    pl.semaphore_wait(barrier, peers)

    for j in range(1, group):
        dec_copy(j).start()
    for p in order:
        for a in range(4):
            for j in range(1, cores):
                in_copy(a, p, j).start()
    own_dec.wait()
    for j in range(1, group):
        dec_copy(j).wait_recv()

    def mine(array, axis):
        result = lax.slice_in_dim(array, 0, heads, axis=axis)
        for j in range(1, cores):
            part = lax.slice_in_dim(array, j * heads, (j + 1) * heads, axis=axis)
            result = jnp.where(core == j, part, result)
        return result

    cum = cum_row = 0.0
    for j in range(cores):
        t_index = lax.broadcasted_iota(jnp.int32, (span, blk), 0)
        s_index = lax.broadcasted_iota(jnp.int32, (span, blk), 1) + j * blk
        tri = jnp.where(t_index >= s_index, 1.0, 0.0).astype(BF16)
        logs = dec[col * cores + j]
        cum += mm(tri, logs, NT)
        cum_row += mm(logs, tri, NT)
    cum, cum_row = mine(cum, 1), mine(cum_row, 0)
    ones = jnp.ones((span, blk), BF16)
    zero = jnp.zeros((dec.shape[1], span), F32)
    before, own, after = zero, zero, zero
    for other in range(cols_n):
        total = zero
        for j in range(cores):
            total += mm(dec[other * cores + j], ones, NT)
        before += jnp.where(other < col, total, 0.0)
        own += jnp.where(other == col, total, 0.0)
        after += jnp.where(other > col, total, 0.0)
    kinds = [jnp.exp(mine(k, 0)) for k in (own, before + own + after, before, after)]
    for i in range(heads):
        cum_b[i] = jnp.broadcast_to(cum[:, i : i + 1], (span, dh))
        cum_t[i] = cum_row[i : i + 1, :]
        for n, kind in enumerate(kinds):
            coef[n, i] = kind[i : i + 1, :]

    def rate(n, index):
        return coef[n, index]

    def row_step(d, g):
        rr, cc, _ = sides(d)

        @pl.when(rr > 0)
        def _():
            a_copy(d, g).wait_recv()

        @pl.when(g < late)
        def _():
            @pl.when(rr < rows_n - 1)
            def _():
                for j in range(per):
                    index = g * per + j
                    a = a_in[d, g, j].astype(F32)
                    a_out[d, g, j] = (rate(1, index) * a + rate(3 - d, index) * kvqo[d, index]).astype(wire)
                a_copy(d, g).start()

            if cols_n > 1:

                @pl.when(cc == 0)
                def _():
                    for j in range(per):
                        index = g * per + j
                        a = a_in[d, g, j].astype(F32)
                        l_out[d, g, j] = (rate(0, index) * a + kvqo[d, index]).astype(wire)
                    l_copy(d, g).start()

                @pl.when(jnp.logical_and(cc == cols_n - 1, rr > 0))
                def _():
                    h_copy(d, g, a_in).start()

        if paired:
            @pl.when(g >= late)
            def _():
                @pl.when(cc > 0)
                def _():
                    l_copy(d, g).wait_recv()

                @pl.when(jnp.logical_and(cc == 0, rr < rows_n - 1))
                def _():
                    h_copy(d, g, h_out).wait_recv()

                @pl.when(rr < rows_n - 1)
                def _():
                    for j in range(per):
                        index = g * per + j
                        met = jnp.where(
                            cc == 0, h_in[d, g, j].astype(F32), rate(0, index) * l_in[d, g, j].astype(F32)
                        )
                        grown = rate(1, index) * a_in[d, g, j].astype(F32) + rate(3 - d, index) * kvqo[d, index]
                        a_out[d, g, j] = (grown + met).astype(wire)
                    a_copy(d, g).start()

    def meet(d, g):
        rr, cc, _ = sides(d)

        @pl.when(cc == 0)
        def _():
            for j in range(per):
                l_out[d, g, j] = kvqo[d, g * per + j].astype(wire)
            l_copy(d, g).start()

        @pl.when(jnp.logical_and(cc > 0, rr < rows_n - 1))
        def _():
            for j in range(per):
                h_out[d, g, j] = kvqo[d, g * per + j].astype(wire)
            h_copy(d, g, h_out).start()

    def col_step(d, g):
        rr, cc, _ = sides(d)
        if cols_n > 1:

            @pl.when(cc > 0)
            def _():
                l_copy(d, g).wait_recv()

        if cols_n > 2:

            @pl.when(jnp.logical_and(cc > 0, cc < cols_n - 1))
            def _():
                for j in range(per):
                    index = g * per + j
                    a = l_in[d, g, j].astype(F32) + rate(2 + d, index) * a_in[d, g, j].astype(F32)
                    l_out[d, g, j] = (rate(0, index) * a + kvqo[d, index]).astype(wire)
                l_copy(d, g).start()

        if cols_n > 1:

            @pl.when(jnp.logical_and(cc < cols_n - 1, rr > 0))
            def _():
                h_copy(d, g, h_out).wait_recv()

        if cols_n > 2:

            @pl.when(jnp.logical_and(jnp.logical_and(cc > 0, cc < cols_n - 1), rr > 0))
            def _():
                for j in range(per):
                    h_out[d, g, j] = (h_in[d, g, j].astype(F32) + a_in[d, g, j].astype(F32)).astype(wire)
                h_copy(d, g, h_out).start()

    def carried(d, g, j):
        index = g * per + j
        both = a_in[d, g, j].astype(F32) + jnp.where(g < late, h_in[d, g, j].astype(F32), 0.0)
        return (l_in[d, g, j].astype(F32) + rate(2 + d, index) * both).astype(BF16)

    def first(i, _):
        g = (i + late) % chunks

        @pl.when(g % (chunks // pieces) == 0)
        def _():
            p = g // (chunks // pieces)
            for a in range(4):
                own_copy(a, p).wait()
                for j in range(1, cores):
                    in_copy(a, p, j).wait_recv()

        for j in range(per):
            index = g * per + j
            cum_h = cum_b[index]
            keep = jnp.exp(cum_h[span - 1 : span, :] - cum_h)
            rising = jnp.exp(cum_h)
            rise[index] = rising
            kept[index] = keep
            weighted_v = (head_rows(1, index).astype(F32) * keep).astype(BF16)
            weighted_q = (head_rows(2, index).astype(F32) * rising).astype(BF16)
            kvqo[0, index] = mm(head_rows(0, index), weighted_v, TN)
            kvqo[1, index] = mm(weighted_q, head_rows(3, index), TN)
        for d in range(2):

            @pl.when(jnp.logical_and(sides(d)[0] == 0, g < late))
            def _():
                row_step(d, g)

            if paired:

                @pl.when(g >= late)
                def _():
                    meet(d, g)

        return 0

    lax.fori_loop(0, chunks, first, 0)

    def within(g):
        lower = lax.broadcasted_iota(jnp.int32, (span, span), 0) >= lax.broadcasted_iota(
            jnp.int32, (span, span), 1
        )
        for j in range(per):
            index = g * per + j
            k, v, q, o = (head_rows(a, index) for a in range(4))
            mask = jnp.where(lower, jnp.exp(jnp.minimum(cum_b[index] - cum_t[index], 0.0)), 0.0)
            vscore = (mm(o, v, NT) * mask).astype(BF16)
            qscore = (mm(q, k, NT) * mask).astype(BF16)
            local[0, index] = mm(vscore, k, NN)
            local[1, index] = mm(vscore, q, TN)
            local[2, index] = mm(qscore, o, TN)

    def sent(g):
        for d in range(2):
            rr, cc, _ = sides(d)

            @pl.when(rr < rows_n - 1)
            def _():
                a_copy(d, g).wait_send()

            if cols_n > 1:

                @pl.when(cc < cols_n - 1)
                def _():
                    l_copy(d, g).wait_send()

                @pl.when(jnp.logical_and(cc > 0, jnp.where(g < late, rr > 0, rr < rows_n - 1)))
                def _():
                    h_copy(d, g, h_out).wait_send()

    def close(g, _):
        for n in range(3):
            out_copy(n, g).wait()
            for j in range(1, cores):
                back_copy(n, g, j).wait_send()
                back_copy(n, g, j).wait_recv()
        return 0

    def last(g):
        @pl.when(g < late)
        def _():
            for d in range(2):
                col_step(d, g)

        sent(g)
        for j in range(per):
            index = g * per + j
            state = carried(0, g, j)
            suffix = carried(1, g, j)
            rising, keep = rise[index], kept[index]
            found = (
                local[0, index] + rising * mm(head_rows(3, index), state, NT),
                local[1, index] + keep * mm(head_rows(1, index), suffix, NT),
                local[2, index] + keep * mm(head_rows(0, index), suffix, NN),
            )
            for n in range(3):
                place_at = pl.ds(pl.multiple_of(index * dh, dh), dh)
                grads[n, :, :, place_at] = found[n].astype(BF16).reshape(cores, blk, dh)
        @pl.when(g % joint == joint - 1)
        def _():
            pair = g // joint
            for n in range(3):
                for j in range(1, cores):
                    back_copy(n, pair, j).start()
                out_copy(n, pair).start()

            @pl.when(pair >= 1)
            def _():
                close(pair - 1, 0)

    def open_chain(g, _):
        for d in range(2):

            @pl.when(sides(d)[0] == 0)
            def _():
                row_step(d, g)

        return 0

    if paired:
        lax.fori_loop(late, chunks, open_chain, 0)
    upper = jnp.where(2 * row >= rows_n, 1, 0)

    def second(g, _):
        for i in range(2):
            d = (upper + i) % 2
            at = g - i * behind

            @pl.when(jnp.logical_and(sides(d)[0] > 0, jnp.logical_and(at >= 0, at < chunks)))
            def _():
                row_step(d, at)

        @pl.when(g < chunks)
        def _():
            within(g)

        @pl.when(g >= lag)
        def _():
            last(g - lag)

        return 0

    for j in range(1, group):
        dec_copy(j).wait_send()
    for p in range(pieces):
        for a in range(4):
            for j in range(1, cores):
                in_copy(a, p, j).wait_send()
    lax.fori_loop(0, chunks + lag, second, 0)

    close(chunks // joint - 1, 0)


def solution(mesh):
    count, cores = mesh.shape["seq"], mesh.shape["head"]
    cols_n = max(c for c in range(1, count + 1) if count % c == 0 and c * c <= count)
    rows_n = count // cols_n
    wire = BF16 if rows_n + cols_n <= 8 else F32

    def per_device(queries, keys, values, out_grad, decay_log):
        blk, model = queries.shape
        all_heads = decay_log.shape[1]
        heads, dh = all_heads // cores, model // all_heads
        per, pieces, behind, lag = 2, 4, 2, 8
        paired = 2 if cols_n == 2 else 0
        chunks = heads // per
        span, group = cores * blk, cols_n * cores
        sizes = (rows_n, cols_n, cores, heads, dh, per, pieces, behind, lag, paired)
        states = pltpu.VMEM((2, chunks, per, dh, dh), wire)
        pair = pltpu.SemaphoreType.DMA((2, chunks))
        return pl.pallas_call(
            functools.partial(kernel, sizes),
            out_shape=[jax.ShapeDtypeStruct((blk, model), BF16)] * 3,
            in_specs=[pl.BlockSpec(memory_space=pl.ANY)] * 5,
            out_specs=[pl.BlockSpec(memory_space=pl.ANY)] * 3,
            scratch_shapes=[
                pltpu.VMEM((4, cores, blk, heads * dh), BF16),
                pltpu.VMEM((group, all_heads, blk), BF16),
                pltpu.VMEM((heads, span, dh), F32),
                pltpu.VMEM((heads, 1, span), F32),
                pltpu.VMEM((heads, span, dh), F32),
                pltpu.VMEM((heads, span, dh), F32),
                pltpu.VMEM((4, heads, 1, span), F32),
                pltpu.VMEM((2, heads, dh, dh), F32),
                states, states, states, states, states, states,
                pltpu.VMEM((3, heads, span, dh), F32),
                pltpu.VMEM((3, cores, blk, heads * dh), BF16),
                pltpu.SemaphoreType.DMA((4, pieces)),
                pltpu.SemaphoreType.DMA((cores - 1, 4, pieces)),
                pltpu.SemaphoreType.DMA((cores - 1, 4, pieces)),
                pltpu.SemaphoreType.DMA,
                pltpu.SemaphoreType.DMA((group - 1,)),
                pltpu.SemaphoreType.DMA((group - 1,)),
                pair, pair, pair, pair, pair, pair,
                pltpu.SemaphoreType.DMA((3, chunks)),
                pltpu.SemaphoreType.DMA((cores - 1, 3, chunks)),
                pltpu.SemaphoreType.DMA((cores - 1, 3, chunks)),
            ],
            compiler_params=pltpu.CompilerParams(
                collective_id=0, has_side_effects=True, vmem_limit_bytes=63 * 1024 * 1024
            ),
            cost_estimate=pl.CostEstimate(
                flops=20 * heads * span * dh * dh, bytes_accessed=14 * blk * model, transcendentals=0
            ),
        )(queries, keys, values, out_grad, decay_log.T)

    rows = P(("parts", "seq", "head"), None)
    return jax.shard_map(
        per_device, mesh=mesh, in_specs=(rows,) * 5, out_specs=(rows,) * 3, check_vma=False
    )
```
